32 devices in a mesh: sec: 2 (over y), dev: 16 (over z, x, core).
Axes of the slice: x: 2, y: 2, z: 4, core: 2. Of those that a mesh axis runs over, the one named last changes fastest.
Arguments:
- hidden_in: bfloat16 [1024, 4096], P(('sec', 'dev')), may hold values from -6 to 6
- routes: int32 [1024, 8], P(('sec', 'dev')), may hold values from 0 to 15, all different within a row; in each aligned block of 32 rows (0 to 31, 32 to 63, ...) at most 32 rows name the same one
- scores: float32 [1024, 8], P(('sec', 'dev')), may hold values from 0.05 to 1
- w_gate: bfloat16 [16, 4096, 1536], P('dev', None, 'sec'), may hold values from -0.09375 to 0.09375
- w_up: bfloat16 [16, 4096, 1536], P('dev', None, 'sec'), may hold values from -0.09375 to 0.09375
- w_down: bfloat16 [16, 1536, 4096], P('dev', 'sec'), may hold values from -0.15625 to 0.15625
Outputs:
- mixed: bfloat16 [1024, 4096], P(('sec', 'dev'))
The draws below stay inside these ranges and needn't reach their ends.
Inputs may be any that keep to these rules, and one draw needn't show every extreme that they name: `routes`: each row names 8 different experts; among the rows of one device no expert is named by more than 32 rows, and in every draw some expert is named by exactly 32 rows of some device.
All inputs are finite; a program needn't handle non-finite values.
Results may differ from the reference program's by a relative error of at most 0.017.
Values may be sent and summed in bfloat16 or wider, within the bound.
No kernel may reach another device: no remote copies, remote signals or barrier semaphores. Data moves between devices by JAX's collectives and lax.ppermute only.
A program may use at most 128 MiB of HBM per device.

```python
import math
import jax
import jax.numpy as jnp
import numpy as np
from jax import lax

D = 4096
FF = 1536
TOP = 8
ROWS_DEV = 32
EXPERTS = 16
CAP = 32
TOKENS = 1024
N_SEC = 2
N_DEV = 16


def shard_levels(stream_key, dims, shards, low, top_value):
    gain = 1.0
    for axis_at, shards_of in shards:
        heights = jax.random.uniform(jax.random.fold_in(jax.random.fold_in(stream_key, 6), axis_at), (shards_of,), jnp.float32, low / len(shards), top_value / len(shards))
        gain = gain * jnp.repeat(jnp.exp(heights), dims[axis_at] // shards_of).reshape((-1,) + (1,) * (len(dims) - 1 - axis_at))
    return gain


def deal_out(stream_key, own, number, rows, amount, top, most, skew):
    sequence = jax.random.permutation(stream_key, amount)
    crowded, usual = portions_of(amount, rows * top, most, skew, True), portions_of(amount, rows * top, most, skew, False)
    places = jnp.arange(amount)

    def named(lengths, offset_by):
        used = int((lengths > 0).sum())
        fixed = max(1, used // 4)
        passed = fixed + (places - fixed + offset_by * (used - fixed)) % max(1, amount - fixed)
        return jnp.zeros((amount,), jnp.int32).at[sequence[jnp.where(places < fixed, places, passed)]].set(jnp.asarray(lengths, jnp.int32))

    lengths = jnp.where(number % 4 == 0, named(crowded, number // 4), named(usual, number - number // 4 - 1))
    mixed = jax.random.permutation(jax.random.fold_in(own, 3), amount)
    donor, receiver = mixed[0:amount // 2 * 2:2], mixed[1:amount // 2 * 2:2]
    room = jnp.minimum(lengths[donor] - 1, most - lengths[receiver]) // 2
    room = jnp.where((donor == sequence[0]) | (receiver == sequence[0]) | (lengths[receiver] == 0), 0, jnp.maximum(room, 0))
    passed = jax.random.randint(jax.random.fold_in(own, 4), (amount // 2,), 0, 1 << 20) % (room + 1)
    lengths = lengths.at[donor].add(-passed).at[receiver].add(passed)
    members = jnp.searchsorted(jnp.cumsum(lengths), jnp.arange(rows * top), side="right").astype(jnp.int32)
    grid = members.reshape(top, rows).T
    grid = grid[jax.random.permutation(jax.random.fold_in(own, 1), rows)]
    offset_by = jax.random.randint(jax.random.fold_in(own, 2), (rows, 1), 0, top)
    return jnp.take_along_axis(grid, (jnp.arange(top)[None, :] + offset_by) % top, axis=1)


def portions_of(amount, total, bound, skew, full):
    weights = [(1 << 20) // math.isqrt(standing ** skew) + 1 for standing in range(1, amount + 1)]
    largest = bound if full else min(bound, max(-(-total // amount), total * weights[0] // sum(weights)))
    least = 1 if total - largest >= amount - 1 else 0
    holding, rest = [largest] + [least] * (amount - 1), total - largest - least * (amount - 1)
    while rest > 0:
        free = [i for i in range(1, amount) if holding[i] < largest] or [i for i in range(1, amount) if holding[i] < bound]
        mass, remaining = sum([weights[i] for i in free]), rest
        for i in free:
            addition = min(bound - holding[i], max(1, remaining * weights[i] // mass), rest)
            holding[i] = holding[i] + addition
            rest = rest - addition
    return np.array(holding)


def centred(key, extent, spread, reach, shards=(), kind=jnp.bfloat16):
    loudness = shard_levels(key, extent, shards, -0.22, 0.18) if shards else 1.0
    values = jax.random.normal(key, extent, jnp.float32) * spread * loudness
    return jnp.minimum(jnp.maximum(values, -reach), reach).astype(kind)


def setup_inputs(seed: int = 0) -> dict:
    splits = jax.random.split(jax.random.key(seed), 7)
    hidden_in = centred(splits[0], (TOKENS, D), 1.0, 6.0, ((0, 32),))
    routes_keys = jax.random.split(jax.random.fold_in(splits[1], 1), TOKENS // ROWS_DEV)
    routes_turns = jax.random.permutation(jax.random.fold_in(splits[1], 3), TOKENS // ROWS_DEV)
    routes = jax.vmap(lambda own, number: deal_out(jax.random.fold_in(splits[1], 2), own, number, ROWS_DEV, EXPERTS, TOP, CAP, 2))(routes_keys, routes_turns).reshape((TOKENS, TOP))
    scores = jnp.clip(jnp.exp(math.log(1.0) - 2.9957323 * jax.random.uniform(splits[2], (TOKENS, TOP), jnp.float32) ** shard_levels(splits[2], (TOKENS, TOP), ((0, 32),), -0.2, 0.2)), 0.05, 1.0)
    w_gate = centred(splits[3], (EXPERTS, D, FF), D ** -0.5, 0.09375, ((0, 16), (2, 2)))
    w_up = centred(splits[4], (EXPERTS, D, FF), D ** -0.5, 0.09375, ((0, 16), (2, 2)))
    w_down = centred(splits[5], (EXPERTS, FF, D), FF ** -0.5, 0.15625, ((0, 16), (1, 2)))
    return dict(hidden_in=hidden_in, routes=routes, scores=scores, w_gate=w_gate, w_up=w_up, w_down=w_down)


def reference(hidden_in, routes, scores, w_gate, w_up, w_down):
    values = hidden_in.astype(jnp.float32)
    normed = (values * lax.rsqrt(lax.optimization_barrier(jnp.mean(values * values, -1, keepdims=True)) + 1e-06)).astype(jnp.bfloat16)
    shares = scores / lax.optimization_barrier(jnp.sum(scores, -1, keepdims=True))
    most_rows = N_SEC * N_DEV * CAP
    highest = lax.Precision.HIGHEST

    def per_expert(summed, expert):
        matches = routes == expert
        weight = lax.optimization_barrier(jnp.sum(jnp.where(matches, shares, jnp.float32(0.0)), -1))
        used = jnp.any(matches, -1)
        indices = jnp.nonzero(used, size=most_rows, fill_value=0)[0].astype(jnp.int32)
        taken = normed[indices].astype(jnp.float32)
        gate_part = jnp.dot(taken, w_gate[expert].astype(jnp.float32), precision=highest)
        up_part = jnp.dot(taken, w_up[expert].astype(jnp.float32), precision=highest)
        hidden_part = (jax.nn.silu(gate_part) * up_part).astype(jnp.bfloat16)
        hidden_part = lax.optimization_barrier(hidden_part).astype(jnp.float32)
        output = jnp.dot(hidden_part, w_down[expert].astype(jnp.float32), precision=highest).astype(jnp.bfloat16)
        output = lax.optimization_barrier(output).astype(jnp.float32)
        live_rows = jnp.arange(most_rows, dtype=jnp.int32) < jnp.sum(used.astype(jnp.int32))
        contrib = jnp.where(live_rows[:, None], output * weight[indices][:, None], jnp.float32(0.0))
        return (summed.at[indices].add(contrib), None)
    start_sum = jnp.zeros(hidden_in.shape, jnp.float32)
    summed, _ = lax.scan(per_expert, start_sum, jnp.arange(EXPERTS, dtype=jnp.int32))
    return summed.astype(jnp.bfloat16)
```

```python
import jax
import jax.numpy as jnp
from jax import lax
from jax.sharding import PartitionSpec as P

BOTH = ("sec", "dev")
CORE, X, ZA, ZB, Y = 1, 2, 4, 8, 16
GATHER = (
    (ZB, 0),
    (X, 0),
    (Y, 0),
    (ZA, 0),
    (X, Y),
    (Y, ZA),
    (ZA, X),
    (X, ZB),
    (Y, ZB),
    (ZA, ZB),
    (X, Y | ZA),
    (X, Y | ZB),
    (Y, ZA | ZB),
    (ZA, X | ZB),
    (Y, X | ZA | ZB),
)


def normalise(hidden_in):
    values = hidden_in.astype(jnp.float32)
    return (values * lax.rsqrt(jnp.mean(values * values, -1, keepdims=True) + 1e-06)).astype(
        jnp.bfloat16
    )


def swap(block, mask, devices):
    return lax.ppermute(block, BOTH, [(i, i ^ mask) for i in range(devices)])


def expert(rows, w_gate, w_up, w_down):
    gate_part = jnp.dot(rows, w_gate, preferred_element_type=jnp.float32)
    up_part = jnp.dot(rows, w_up, preferred_element_type=jnp.float32)
    hidden_part = (jax.nn.silu(gate_part) * up_part).astype(jnp.bfloat16)
    return jnp.dot(hidden_part, w_down, preferred_element_type=jnp.float32)


def spread(hidden_in, routes, scores, w_gate, w_up, w_down):
    rows_dev, model_width = hidden_in.shape
    experts = lax.axis_size("dev")
    devices = experts * lax.axis_size("sec")
    shares = scores / jnp.sum(scores, -1, keepdims=True)
    table = jnp.sum(
        jnp.where(
            routes[:, :, None] == jnp.arange(experts, dtype=jnp.int32), shares[:, :, None], 0.0
        ),
        1,
    )
    terms = []
    for _ in range(3):
        term = table.astype(jnp.bfloat16)
        terms.append(term)
        table = table - term.astype(jnp.float32)
    blank = jnp.zeros((rows_dev, -3 * experts % 128), jnp.bfloat16)
    held = {0: jnp.concatenate([normalise(hidden_in), *terms, blank], 1)}
    mine = (jnp.arange(experts) == lax.axis_index("dev")).astype(jnp.float32)

    for link, block in GATHER:
        held[block ^ link] = swap(held[block], link, devices)
    for block in [m for m in held]:
        held[block ^ CORE] = swap(held[block], CORE, devices)

    sums = {}
    for high in (0, ZB):
        group = [m for m in range(devices) if m & ZB == high]
        rows = jnp.concatenate([held[m] for m in group], 0)
        table = rows[:, model_width : model_width + 3 * experts].astype(jnp.float32)
        weight = jnp.sum(table.reshape(-1, 3, experts) * mine, (1, 2))
        out = expert(rows[:, :model_width], w_gate[0], w_up[0], w_down[0]) * weight[:, None]
        out = out.astype(jnp.bfloat16).reshape(len(group), rows_dev, model_width)
        for at, m in enumerate(group):
            sums[m] = out[at]

    pending = {}
    for m in range(devices):
        if not m & CORE:
            pending[m] = [sums[m], swap(sums[m ^ CORE], CORE, devices)]

    def total(m):
        return sum(part.astype(jnp.float32) for part in pending[m]).astype(jnp.bfloat16)

    for link, block in reversed(GATHER):
        pending[block].append(swap(total(block ^ link), link, devices))
    return total(0)


def dispatch(hidden_in, routes, scores, w_gate, w_up, w_down):
    rows_dev, model_width = hidden_in.shape
    top_k = routes.shape[1]
    experts = lax.axis_size("dev")
    slots_dev = 2 * rows_dev * top_k // experts
    slot_rows = experts * slots_dev
    normed = normalise(hidden_in)
    shares = scores / jnp.sum(scores, -1, keepdims=True)
    chosen = routes.reshape(-1)
    onehot = (chosen[:, None] == jnp.arange(experts, dtype=jnp.int32)[None, :]).astype(jnp.int32)
    before = jnp.cumsum(onehot, 0) - onehot
    position = jnp.sum(before * onehot, 1)
    target = (chosen * slots_dev + position).reshape(rows_dev, top_k)
    places = jnp.arange(slot_rows, dtype=jnp.int32)
    picker = jnp.any(target[None, :, :] == places[:, None, None], -1).astype(jnp.bfloat16)
    outgoing = jnp.dot(picker, normed, preferred_element_type=jnp.float32).astype(jnp.bfloat16)
    outgoing = outgoing.reshape(experts, slots_dev, model_width)
    arrived = lax.all_to_all(outgoing, "dev", split_axis=0, concat_axis=0, tiled=True).reshape(
        slot_rows, model_width
    )
    paired = lax.all_gather(arrived, "sec", axis=0, tiled=True)
    result = lax.psum_scatter(
        expert(paired, w_gate[0], w_up[0], w_down[0]).astype(jnp.bfloat16),
        "sec",
        scatter_dimension=0,
        tiled=True,
    )
    expert_out = result.reshape(experts, slots_dev, model_width)
    returned = lax.all_to_all(expert_out, "dev", split_axis=0, concat_axis=0, tiled=True).reshape(
        slot_rows, model_width
    )
    picked = jnp.take(returned, target.reshape(-1), axis=0).reshape(rows_dev, top_k, model_width)
    combined = jnp.einsum("rk,rkd->rd", shares, picked.astype(jnp.float32))
    return combined.astype(jnp.bfloat16)


def on_device(hidden_in, routes, scores, *weights):
    experts, halves = lax.axis_size("dev"), lax.axis_size("sec")
    roomy = 2 * routes.shape[1] >= experts
    plan = spread if roomy and (halves, experts) == (2, 16) else dispatch
    return plan(hidden_in, routes, scores, *weights)


def solution(mesh):
    placed = (
        P(("sec", "dev"), None),
        P(("sec", "dev"), None),
        P(("sec", "dev"), None),
        P("dev", None, "sec"),
        P("dev", None, "sec"),
        P("dev", "sec", None),
    )
    return jax.shard_map(
        on_device, mesh=mesh, in_specs=placed, out_specs=P(("sec", "dev"), None), check_vma=False
    )
```

```python
import functools

import jax
import jax.numpy as jnp
from jax import lax
from jax.experimental import pallas as pl
from jax.experimental.pallas import tpu as pltpu
from jax.sharding import PartitionSpec as P

BOTH = ("sec", "dev")
CORE, X, ZA, ZB, Y = 1, 2, 4, 8, 16
NEAR = (0, ZA, X, Y)
FAR = (X | Y, X | ZA, Y | ZA, X | Y | ZA)
TERMS = 3
VMEM = pl.BlockSpec(memory_space=pltpu.VMEM)


def normalise(hidden_in):
    values = hidden_in.astype(jnp.float32)
    return (values * lax.rsqrt(jnp.mean(values * values, -1, keepdims=True) + 1e-06)).astype(
        jnp.bfloat16
    )


def swap(block, mask, devices):
    return lax.ppermute(block, BOTH, [(i, i ^ mask) for i in range(devices)])


def expert(rows, w_gate, w_up, w_down):
    gate_part = jnp.dot(rows, w_gate, preferred_element_type=jnp.float32)
    up_part = jnp.dot(rows, w_up, preferred_element_type=jnp.float32)
    hidden_part = (jax.nn.silu(gate_part) * up_part).astype(jnp.bfloat16)
    return jnp.dot(hidden_part, w_down, preferred_element_type=jnp.float32)


def local(body, outs, operands, scratch=(), limit=8, **cost):
    return pl.pallas_call(
        body,
        out_shape=[jax.ShapeDtypeStruct(shape, jnp.bfloat16) for shape in outs],
        in_specs=[VMEM] * len(operands),
        out_specs=[VMEM] * len(outs),
        scratch_shapes=list(scratch),
        compiler_params=pltpu.CompilerParams(vmem_limit_bytes=limit * 2**20),
        cost_estimate=pl.CostEstimate(**{"flops": 0, "transcendentals": 0, "bytes_accessed": 0, **cost}),
    )(*operands)


def prepare_body(experts, hidden_ref, routes_ref, scores_ref, out_ref):
    width = hidden_ref.shape[1]
    out_ref[:, :width] = normalise(hidden_ref[...])
    scores = scores_ref[...]
    shares = scores / jnp.sum(scores, -1, keepdims=True)
    lanes = lax.broadcasted_iota(jnp.int32, (hidden_ref.shape[0], 128), 1)
    table = jnp.zeros(lanes.shape, jnp.float32)
    for k in range(routes_ref.shape[1]):
        named = routes_ref[:, k : k + 1] == lanes % experts
        table = table + jnp.where(named, shares[:, k : k + 1], 0.0)
    packed = jnp.zeros(lanes.shape, jnp.float32)
    for at in range(TERMS):
        term = table.astype(jnp.bfloat16).astype(jnp.float32)
        packed = jnp.where(lanes // experts == at, term, packed)
        table = table - term
    out_ref[:, width:] = packed.astype(jnp.bfloat16)


def prepare(hidden_in, routes, scores, experts):
    rows, width = hidden_in.shape
    return local(
        functools.partial(prepare_body, experts), [(rows, width + 128)], (hidden_in, routes, scores)
    )[0]


def expert_body(count, mine_ref, *refs):
    blocks, (gate_ref, up_ref, down_ref), outs = refs[:count], refs[count : count + 3], refs[count + 3 : count + 5]
    rows_ref, hidden_ref = refs[count + 5 :]
    rows, width = blocks[0].shape[0], down_ref.shape[1]
    shares = []
    for at, block in enumerate(blocks):
        rows_ref[at * rows : (at + 1) * rows, :] = block[:, :width]
        shares.append(jnp.sum(block[:, width:].astype(jnp.float32) * mine_ref[...], -1, keepdims=True))
    weight = jnp.concatenate(shares, 0)
    for at in range(0, gate_ref.shape[1], 256):
        cols = slice(at, at + 256)
        gate_part = jnp.dot(rows_ref[...], gate_ref[:, cols], preferred_element_type=jnp.float32)
        up_part = jnp.dot(rows_ref[...], up_ref[:, cols], preferred_element_type=jnp.float32)
        hidden_ref[:, cols] = (gate_part / (1.0 + jnp.exp(-gate_part)) * up_part).astype(jnp.bfloat16)
    half = count // 2 * rows

    @pl.loop(0, width // 1024)
    def _(at):
        cols = pl.ds(pl.multiple_of(at * 1024, 1024), 1024)
        out = jnp.dot(hidden_ref[...], down_ref[:, cols], preferred_element_type=jnp.float32) * weight
        outs[0][:, cols] = out[:half].astype(jnp.bfloat16)
        outs[1][:, cols] = out[half:].astype(jnp.bfloat16)


def expert_rows(blocks, mine, w_gate, w_up, w_down):
    count, rows = len(blocks), blocks[0].shape[0]
    width, units = w_down.shape[1], w_gate.shape[1]
    return local(
        functools.partial(expert_body, count),
        [(count // 2 * rows, width)] * 2,
        (mine, *blocks, w_gate, w_up, w_down),
        [pltpu.VMEM((count * rows, width), jnp.bfloat16), pltpu.VMEM((count * rows, units), jnp.bfloat16)],
        flops=6 * count * rows * width * units,
        bytes_accessed=2 * count * rows * width,
    )


def add_body(plan, count, *refs):
    for out, parts in zip(refs[count:], plan):
        rows = out.shape[0]
        total = 0.0
        for ref, at in parts:
            total = total + refs[ref][at * rows : (at + 1) * rows, :].astype(jnp.float32)
        out[...] = total.astype(jnp.bfloat16)


def add_up(plan, arrays, rows):
    shapes = [(rows, arrays[0].shape[1])] * len(plan)
    return local(functools.partial(add_body, plan, len(arrays)), shapes, arrays, limit=4)


def spread(hidden_in, routes, scores, w_gate, w_up, w_down):
    rows = hidden_in.shape[0]
    experts = lax.axis_size("dev")
    devices = experts * lax.axis_size("sec")
    lanes = jnp.arange(128)
    mine = (lanes % experts == lax.axis_index("dev")) & (lanes < TERMS * experts)
    mine = mine.astype(jnp.float32)[None, :]
    weights = (mine, w_gate[0], w_up[0], w_down[0])
    held = {0: prepare(hidden_in, routes, scores, experts)}

    def send(link, block):
        held[block ^ link] = swap(held[block], link, devices)

    send(ZB, 0)
    for top in (0, ZB):
        for link in (ZA, X, Y, X | Y):
            send(link, top)
        send(X, top | ZA)
        send(Y, top | ZA)
        send(ZA, top | X | Y)
    for m in list(held):
        send(CORE, m)

    outs = {}
    for top in (0, ZB):
        for at, group in enumerate((NEAR, FAR)):
            group = [top | m for m in group]
            own, other = expert_rows([held[m] for m in group] + [held[m ^ CORE] for m in group], *weights)
            outs[top, at] = own, swap(other, CORE, devices)

    ends = []
    for top in (0, ZB):
        far, near = outs[top, 1], outs[top, 0]
        xa, ya, xya = add_up([[(0, at), (1, at)] for at in (1, 2, 3)], far, rows)
        xa, ya, xya = swap(xa, X, devices), swap(ya, Y, devices), swap(xya, ZA, devices)
        a, x, y, xy = add_up(
            [
                [(0, 1), (1, 1), (4, 0), (5, 0)],
                [(0, 2), (1, 2)],
                [(0, 3), (1, 3)],
                [(2, 0), (3, 0), (6, 0)],
            ],
            (*near, *far, xa, ya, xya),
            rows,
        )
        ends.append((*near, swap(a, ZA, devices), swap(x, X, devices), swap(y, Y, devices), swap(xy, X | Y, devices)))
    whole = [(at, 0) for at in range(6)]
    top = add_up([whole], ends[1], rows)[0]
    return add_up([[*whole, (6, 0)]], (*ends[0], swap(top, ZB, devices)), rows)[0]


def dispatch(hidden_in, routes, scores, w_gate, w_up, w_down):
    rows_dev, model_width = hidden_in.shape
    top_k = routes.shape[1]
    experts = lax.axis_size("dev")
    slots_dev = 2 * rows_dev * top_k // experts
    slot_rows = experts * slots_dev
    normed = normalise(hidden_in)
    shares = scores / jnp.sum(scores, -1, keepdims=True)
    chosen = routes.reshape(-1)
    onehot = (chosen[:, None] == jnp.arange(experts, dtype=jnp.int32)[None, :]).astype(jnp.int32)
    before = jnp.cumsum(onehot, 0) - onehot
    position = jnp.sum(before * onehot, 1)
    target = (chosen * slots_dev + position).reshape(rows_dev, top_k)
    places = jnp.arange(slot_rows, dtype=jnp.int32)
    picker = jnp.any(target[None, :, :] == places[:, None, None], -1).astype(jnp.bfloat16)
    outgoing = jnp.dot(picker, normed, preferred_element_type=jnp.float32).astype(jnp.bfloat16)
    outgoing = outgoing.reshape(experts, slots_dev, model_width)
    arrived = lax.all_to_all(outgoing, "dev", split_axis=0, concat_axis=0, tiled=True).reshape(
        slot_rows, model_width
    )
    paired = lax.all_gather(arrived, "sec", axis=0, tiled=True)
    result = lax.psum_scatter(
        expert(paired, w_gate[0], w_up[0], w_down[0]).astype(jnp.bfloat16),
        "sec",
        scatter_dimension=0,
        tiled=True,
    )
    expert_out = result.reshape(experts, slots_dev, model_width)
    returned = lax.all_to_all(expert_out, "dev", split_axis=0, concat_axis=0, tiled=True).reshape(
        slot_rows, model_width
    )
    picked = jnp.take(returned, target.reshape(-1), axis=0).reshape(rows_dev, top_k, model_width)
    combined = jnp.einsum("rk,rkd->rd", shares, picked.astype(jnp.float32))
    return combined.astype(jnp.bfloat16)


def on_device(hidden_in, routes, scores, *weights):
    experts, halves = lax.axis_size("dev"), lax.axis_size("sec")
    roomy = 2 * routes.shape[1] >= experts
    plan = spread if roomy and (halves, experts) == (2, 16) else dispatch
    return plan(hidden_in, routes, scores, *weights)


def solution(mesh):
    placed = (
        P(("sec", "dev"), None),
        P(("sec", "dev"), None),
        P(("sec", "dev"), None),
        P("dev", None, "sec"),
        P("dev", None, "sec"),
        P("dev", "sec", None),
    )
    return jax.shard_map(
        on_device, mesh=mesh, in_specs=placed, out_specs=P(("sec", "dev"), None), check_vma=False
    )
```

```python
import functools

import jax
import jax.numpy as jnp
from jax import lax
from jax.experimental import pallas as pl
from jax.experimental.pallas import tpu as pltpu
from jax.sharding import PartitionSpec as P

BOTH = ("sec", "dev")
CORE, X, ZA, ZB, Y = 1, 2, 4, 8, 16
TERMS = 3
VMEM = pl.BlockSpec(memory_space=pltpu.VMEM)


def normalise(hidden_in):
    values = hidden_in.astype(jnp.float32)
    return (values * lax.rsqrt(jnp.mean(values * values, -1, keepdims=True) + 1e-06)).astype(
        jnp.bfloat16
    )


def swap(block, mask, devices):
    return lax.ppermute(block, BOTH, [(i, i ^ mask) for i in range(devices)])


def expert(rows, w_gate, w_up, w_down):
    gate_part = jnp.dot(rows, w_gate, preferred_element_type=jnp.float32)
    up_part = jnp.dot(rows, w_up, preferred_element_type=jnp.float32)
    hidden_part = (jax.nn.silu(gate_part) * up_part).astype(jnp.bfloat16)
    return jnp.dot(hidden_part, w_down, preferred_element_type=jnp.float32)


def local(body, outs, operands, scratch=(), limit=8, **cost):
    return pl.pallas_call(
        body,
        out_shape=[jax.ShapeDtypeStruct(shape, jnp.bfloat16) for shape in outs],
        in_specs=[VMEM] * len(operands),
        out_specs=[VMEM] * len(outs),
        scratch_shapes=list(scratch),
        compiler_params=pltpu.CompilerParams(vmem_limit_bytes=limit * 2**20),
        cost_estimate=pl.CostEstimate(**{"flops": 0, "transcendentals": 0, "bytes_accessed": 0, **cost}),
    )(*operands)


def prepare_body(experts, hidden_ref, routes_ref, scores_ref, out_ref):
    width = hidden_ref.shape[1]
    out_ref[:, :width] = normalise(hidden_ref[...])
    scores = scores_ref[...]
    shares = scores / jnp.sum(scores, -1, keepdims=True)
    lanes = lax.broadcasted_iota(jnp.int32, (hidden_ref.shape[0], 128), 1)
    table = jnp.zeros(lanes.shape, jnp.float32)
    for k in range(routes_ref.shape[1]):
        named = routes_ref[:, k : k + 1] == lanes % experts
        table = table + jnp.where(named, shares[:, k : k + 1], 0.0)
    packed = jnp.zeros(lanes.shape, jnp.float32)
    for at in range(TERMS):
        term = table.astype(jnp.bfloat16).astype(jnp.float32)
        packed = jnp.where(lanes // experts == at, term, packed)
        table = table - term
    out_ref[:, width:] = packed.astype(jnp.bfloat16)


def prepare(hidden_in, routes, scores, experts):
    rows, width = hidden_in.shape
    return local(
        functools.partial(prepare_body, experts), [(rows, width + 128)], (hidden_in, routes, scores)
    )[0]


def expert_body(count, mine_ref, *refs):
    blocks, (gate_ref, up_ref, down_ref), outs = refs[:count], refs[count : count + 3], refs[count + 3 : count + 5]
    rows_ref, hidden_ref = refs[count + 5 :]
    rows, width = blocks[0].shape[0], down_ref.shape[1]
    shares = []
    for at, block in enumerate(blocks):
        rows_ref[at * rows : (at + 1) * rows, :] = block[:, :width]
        shares.append(jnp.sum(block[:, width:].astype(jnp.float32) * mine_ref[...], -1, keepdims=True))
    weight = jnp.concatenate(shares, 0)
    for at in range(0, gate_ref.shape[1], 256):
        cols = slice(at, at + 256)
        gate_part = jnp.dot(rows_ref[...], gate_ref[:, cols], preferred_element_type=jnp.float32)
        up_part = jnp.dot(rows_ref[...], up_ref[:, cols], preferred_element_type=jnp.float32)
        hidden_ref[:, cols] = (gate_part / (1.0 + jnp.exp(-gate_part)) * up_part).astype(jnp.bfloat16)
    half = count // 2 * rows

    @pl.loop(0, width // 1024)
    def _(at):
        cols = pl.ds(pl.multiple_of(at * 1024, 1024), 1024)
        out = jnp.dot(hidden_ref[...], down_ref[:, cols], preferred_element_type=jnp.float32) * weight
        outs[0][:, cols] = out[:half].astype(jnp.bfloat16)
        outs[1][:, cols] = out[half:].astype(jnp.bfloat16)


def expert_rows(blocks, mine, w_gate, w_up, w_down):
    count, rows = len(blocks), blocks[0].shape[0]
    width, units = w_down.shape[1], w_gate.shape[1]
    return local(
        functools.partial(expert_body, count),
        [(count // 2 * rows, width)] * 2,
        (mine, *blocks, w_gate, w_up, w_down),
        [pltpu.VMEM((count * rows, width), jnp.bfloat16), pltpu.VMEM((count * rows, units), jnp.bfloat16)],
        flops=6 * count * rows * width * units,
        bytes_accessed=2 * count * rows * width,
    )


def add_body(plan, count, rows, *refs):
    for out, blocks in zip(refs[count:], plan):
        for at, parts in enumerate(blocks):
            cut = [refs[ref][place * rows : (place + 1) * rows, :] for ref, place in parts]
            if len(cut) > 1:
                cut = [sum(part.astype(jnp.float32) for part in cut).astype(jnp.bfloat16)]
            out[at * rows : (at + 1) * rows, :] = cut[0]


def combine(wanted, pieces, rows):
    plan = [
        [
            [(ref, names.index(m)) for ref, (names, _) in enumerate(pieces) if m in names]
            for m in blocks
        ]
        for blocks in wanted
    ]
    arrays = [array for _, array in pieces]
    width = arrays[0].shape[1]
    outs = local(
        functools.partial(add_body, plan, len(arrays), rows),
        [(len(blocks) * rows, width) for blocks in wanted],
        arrays,
        limit=4,
    )
    return list(zip(wanted, outs))


def spread(hidden_in, routes, scores, w_gate, w_up, w_down):
    rows = hidden_in.shape[0]
    experts = lax.axis_size("dev")
    devices = experts * lax.axis_size("sec")
    lanes = jnp.arange(128)
    mine = (lanes % experts == lax.axis_index("dev")) & (lanes < TERMS * experts)
    mine = mine.astype(jnp.float32)[None, :]
    weights = w_gate[0], w_up[0], w_down[0]

    def send(link, piece):
        names, array = piece
        return tuple(m ^ link for m in names), swap(array, link, devices)

    def sums(group):
        there = swap(group[1], CORE, devices)
        own, other = expert_rows([group[1], there], mine, *weights)
        return [(group[0], own), (group[0], swap(other, CORE, devices))]

    def tie(*pieces):
        arrays = lax.optimization_barrier(tuple(array for _, array in pieces))
        return [(names, array) for (names, _), array in zip(pieces, arrays)]

    start = [0], prepare(hidden_in, routes, scores, experts)
    za, x, y, zb, xy = [send(link, start) for link in (ZA, X, Y, ZB, X | Y)]
    near0, zs, ps = combine(
        [[0, ZA, X, Y], [ZA, ZB], [X | Y, ZB]], [start, za, x, y, zb, xy], rows
    )
    got = [send(X, zs), send(Y, zs), send(ZA, ps), send(X | Y, zb)]
    near0 = sums(near0)
    near0[0], *got = tie(near0[0], xy, zb, *got)
    far0, near1, zab, xyb = combine(
        [
            [X | Y, X | ZA, Y | ZA, X | Y | ZA],
            [ZB, ZA | ZB, X | ZB, Y | ZB],
            [ZA | ZB],
            [X | Y | ZB],
        ],
        got,
        rows,
    )
    got = [send(X, zab), send(Y, zab), send(ZA, xyb)]
    far0 = sums(far0)
    near1 = sums(near1)
    far0[0], near1[0], *got = tie(far0[0], near1[0], xyb, *got)
    (far1,) = combine([[X | Y | ZB, X | ZA | ZB, Y | ZA | ZB, X | Y | ZA | ZB]], got, rows)
    far1 = sums(far1)

    x, y = combine([[X], [Y]], near0, rows)
    end = [*near0, send(X, x), send(Y, y)]
    x, y, xya = combine(
        [[X | ZA, X | ZB], [Y | ZA, Y | ZB], [X | Y | ZA]], [*far0, *near1], rows
    )
    x, y, xya = send(X, x), send(Y, y), send(ZA, xya)
    xa, ya, xyab = combine([[X | ZA | ZB], [Y | ZA | ZB], [X | Y | ZA | ZB]], far1, rows)
    xa, ya, xyab = send(X, xa), send(Y, ya), send(ZA, xyab)
    za, xy = combine([[ZA], [X | Y]], [*near0, *far0, x, y, xya], rows)
    end += [send(ZA, za), send(X | Y, xy)]
    zab, xyb = combine([[ZA | ZB], [X | Y | ZB]], [*near1, *far1, xa, ya, xyab], rows)
    (zb,) = combine([[ZB]], [*near1, x, y, send(ZA, zab), send(X | Y, xyb)], rows)
    return combine([[0]], [*end, send(ZB, zb)], rows)[0][1]


def dispatch(hidden_in, routes, scores, w_gate, w_up, w_down):
    rows_dev, model_width = hidden_in.shape
    top_k = routes.shape[1]
    experts = lax.axis_size("dev")
    slots_dev = 2 * rows_dev * top_k // experts
    slot_rows = experts * slots_dev
    normed = normalise(hidden_in)
    shares = scores / jnp.sum(scores, -1, keepdims=True)
    chosen = routes.reshape(-1)
    onehot = (chosen[:, None] == jnp.arange(experts, dtype=jnp.int32)[None, :]).astype(jnp.int32)
    before = jnp.cumsum(onehot, 0) - onehot
    position = jnp.sum(before * onehot, 1)
    target = (chosen * slots_dev + position).reshape(rows_dev, top_k)
    places = jnp.arange(slot_rows, dtype=jnp.int32)
    picker = jnp.any(target[None, :, :] == places[:, None, None], -1).astype(jnp.bfloat16)
    outgoing = jnp.dot(picker, normed, preferred_element_type=jnp.float32).astype(jnp.bfloat16)
    outgoing = outgoing.reshape(experts, slots_dev, model_width)
    arrived = lax.all_to_all(outgoing, "dev", split_axis=0, concat_axis=0, tiled=True).reshape(
        slot_rows, model_width
    )
    paired = lax.all_gather(arrived, "sec", axis=0, tiled=True)
    result = lax.psum_scatter(
        expert(paired, w_gate[0], w_up[0], w_down[0]).astype(jnp.bfloat16),
        "sec",
        scatter_dimension=0,
        tiled=True,
    )
    expert_out = result.reshape(experts, slots_dev, model_width)
    returned = lax.all_to_all(expert_out, "dev", split_axis=0, concat_axis=0, tiled=True).reshape(
        slot_rows, model_width
    )
    picked = jnp.take(returned, target.reshape(-1), axis=0).reshape(rows_dev, top_k, model_width)
    combined = jnp.einsum("rk,rkd->rd", shares, picked.astype(jnp.float32))
    return combined.astype(jnp.bfloat16)


def on_device(hidden_in, routes, scores, *weights):
    experts, halves = lax.axis_size("dev"), lax.axis_size("sec")
    roomy = 2 * routes.shape[1] >= experts
    plan = spread if roomy and (halves, experts) == (2, 16) else dispatch
    return plan(hidden_in, routes, scores, *weights)


def solution(mesh):
    placed = (
        P(("sec", "dev"), None),
        P(("sec", "dev"), None),
        P(("sec", "dev"), None),
        P("dev", None, "sec"),
        P("dev", None, "sec"),
        P("dev", "sec", None),
    )
    return jax.shard_map(
        on_device, mesh=mesh, in_specs=placed, out_specs=P(("sec", "dev"), None), check_vma=False
    )
```

```python
import functools

import jax
import jax.numpy as jnp
from jax import lax
from jax.experimental import pallas as pl
from jax.experimental.pallas import tpu as pltpu
from jax.sharding import PartitionSpec as P

BOTH = ("sec", "dev")
CORE, X, ZA, ZB, Y = 1, 2, 4, 8, 16
TERMS = 3
VMEM = pl.BlockSpec(memory_space=pltpu.VMEM)


def normalise(hidden_in):
    values = hidden_in.astype(jnp.float32)
    return (values * lax.rsqrt(jnp.mean(values * values, -1, keepdims=True) + 1e-06)).astype(
        jnp.bfloat16
    )


def swap(block, mask, devices):
    return lax.ppermute(block, BOTH, [(i, i ^ mask) for i in range(devices)])


def expert(rows, w_gate, w_up, w_down):
    gate_part = jnp.dot(rows, w_gate, preferred_element_type=jnp.float32)
    up_part = jnp.dot(rows, w_up, preferred_element_type=jnp.float32)
    hidden_part = (jax.nn.silu(gate_part) * up_part).astype(jnp.bfloat16)
    return jnp.dot(hidden_part, w_down, preferred_element_type=jnp.float32)


def local(body, outs, operands, scratch=(), limit=12, after=(), **cost):
    return pl.pallas_call(
        body,
        out_shape=[jax.ShapeDtypeStruct(shape, jnp.bfloat16) for shape in outs],
        in_specs=[VMEM] * len(operands) + [pl.BlockSpec(memory_space=pl.ANY)] * len(after),
        out_specs=[VMEM] * len(outs),
        scratch_shapes=list(scratch),
        compiler_params=pltpu.CompilerParams(vmem_limit_bytes=limit * 2**20),
        cost_estimate=pl.CostEstimate(**{"flops": 0, "transcendentals": 0, "bytes_accessed": 0, **cost}),
    )(*operands, *after)


def prepare_body(experts, hidden_ref, routes_ref, scores_ref, _, out_ref):
    width = hidden_ref.shape[1]
    out_ref[:, :width] = normalise(hidden_ref[...])
    scores = scores_ref[...]
    shares = scores / jnp.sum(scores, -1, keepdims=True)
    lanes = lax.broadcasted_iota(jnp.int32, (hidden_ref.shape[0], 128), 1)
    table = jnp.zeros(lanes.shape, jnp.float32)
    for k in range(routes_ref.shape[1]):
        named = routes_ref[:, k : k + 1] == lanes % experts
        table = table + jnp.where(named, shares[:, k : k + 1], 0.0)
    packed = jnp.zeros(lanes.shape, jnp.float32)
    for at in range(TERMS):
        term = table.astype(jnp.bfloat16).astype(jnp.float32)
        packed = jnp.where(lanes // experts == at, term, packed)
        table = table - term
    out_ref[:, width:] = packed.astype(jnp.bfloat16)


def prepare(hidden_in, routes, scores, experts, after):
    rows, width = hidden_in.shape
    return local(
        functools.partial(prepare_body, experts),
        [(rows, width + 128)],
        (hidden_in, routes, scores),
        after=after,
    )[0]


def fetch_body(count, after_ref, *refs):
    sources, outs, (token_ref, sems) = refs[:count], refs[count : 2 * count], refs[2 * count :]
    token_ref[...] = jnp.zeros(token_ref.shape, token_ref.dtype)
    copies = [pltpu.make_async_copy(sources[at], outs[at], sems.at[at]) for at in range(count)]
    for copy in copies:
        copy.start()
    for copy in copies:
        copy.wait()


def fetch(arrays, after):
    sources = [pltpu.with_memory_space_constraint(a, pltpu.HBM) for a in arrays]
    anywhere = pl.BlockSpec(memory_space=pl.ANY)
    *outs, token = pl.pallas_call(
        functools.partial(fetch_body, len(arrays)),
        out_shape=[pltpu.VMEM(a.shape, a.dtype) for a in arrays]
        + [jax.ShapeDtypeStruct((16, 128), jnp.bfloat16)],
        in_specs=[anywhere] * (1 + len(arrays)),
        out_specs=[VMEM] * (len(arrays) + 1),
        scratch_shapes=[pltpu.SemaphoreType.DMA((len(arrays),))],
        compiler_params=pltpu.CompilerParams(vmem_limit_bytes=4 * 2**20),
    )(after, *sources)
    return [pltpu.with_memory_space_constraint(a, pltpu.VMEM) for a in outs], token


def expert_body(count, mine_ref, *refs):
    blocks, (gate_ref, up_ref, down_ref) = refs[:count], refs[count : count + 3]
    *outs, rows_ref, hidden_ref = refs[count + 3 :]
    width, first = down_ref.shape[1], 0
    shares = []
    for block in blocks:
        rows_ref[first : first + block.shape[0], :] = block[:, :width]
        first += block.shape[0]
        shares.append(jnp.sum(block[:, width:].astype(jnp.float32) * mine_ref[...], -1, keepdims=True))
    weight = jnp.concatenate(shares, 0)
    for at in range(0, gate_ref.shape[1], 256):
        cols = slice(at, at + 256)
        gate_part = jnp.dot(rows_ref[...], gate_ref[:, cols], preferred_element_type=jnp.float32)
        up_part = jnp.dot(rows_ref[...], up_ref[:, cols], preferred_element_type=jnp.float32)
        hidden_ref[:, cols] = (gate_part / (1.0 + jnp.exp(-gate_part)) * up_part).astype(jnp.bfloat16)
    half = first // 2

    @pl.loop(0, width // 1024)
    def _(at):
        cols = pl.ds(pl.multiple_of(at * 1024, 1024), 1024)
        out = jnp.dot(hidden_ref[...], down_ref[:, cols], preferred_element_type=jnp.float32) * weight
        outs[0][:, cols] = out[:half].astype(jnp.bfloat16)
        outs[1][:, cols] = out[half:].astype(jnp.bfloat16)


def expert_rows(blocks, mine, w_gate, w_up, w_down):
    rows = sum(block.shape[0] for block in blocks)
    width, units = w_down.shape[1], w_gate.shape[1]
    return local(
        functools.partial(expert_body, len(blocks)),
        [(rows // 2, width)] * 2,
        (mine, *blocks, w_gate, w_up, w_down),
        [pltpu.VMEM((rows, width), jnp.bfloat16), pltpu.VMEM((rows, units), jnp.bfloat16)],
        flops=6 * rows * width * units,
        bytes_accessed=2 * rows * width,
    )


def add_body(plan, count, rows, *refs):
    for out, blocks in zip(refs[count:], plan):
        for at, parts in enumerate(blocks):
            cut = [refs[ref][place * rows : (place + 1) * rows, :] for ref, place in parts]
            if len(cut) > 1:
                cut = [sum(part.astype(jnp.float32) for part in cut).astype(jnp.bfloat16)]
            out[at * rows : (at + 1) * rows, :] = cut[0]


def combine(wanted, pieces, rows, after=()):
    plan = [
        [
            [(ref, names.index(m)) for ref, (names, _) in enumerate(pieces) if m in names]
            for m in blocks
        ]
        for blocks in wanted
    ]
    arrays = [array for _, array in pieces]
    width = arrays[0].shape[1]
    outs = local(
        functools.partial(add_body, plan, len(arrays) + len(after), rows),
        [(len(blocks) * rows, width) for blocks in wanted],
        arrays,
        limit=4,
        after=after,
    )
    return list(zip(wanted, outs))


def spread(hidden_in, routes, scores, w_gate, w_up, w_down):
    rows = hidden_in.shape[0]
    experts = lax.axis_size("dev")
    devices = experts * lax.axis_size("sec")
    lanes = jnp.arange(128)
    mine = (lanes % experts == lax.axis_index("dev")) & (lanes < TERMS * experts)
    mine = mine.astype(jnp.float32)[None, :]

    def send(link, piece):
        names, array = piece
        return tuple(m ^ link for m in names), swap(array, link, devices)

    def sums(pieces, *beside):
        names = sum((tuple(names) for names, _ in pieces), ())
        here = [array for _, array in pieces]
        there = [swap(array, CORE, devices) for array in here]
        own, other = expert_rows(here + there, mine, *weights)
        own, other, *arrays = lax.optimization_barrier(
            (own, other, *(array for _, array in beside))
        )
        arrived = [(names, array) for (names, _), array in zip(beside, arrays)]
        return [(names, own), (names, swap(other, CORE, devices))], *arrived

    start = [0], prepare(hidden_in, routes, scores, experts, [mine])
    zb, za, x, y, xy = [send(link, start) for link in (ZB, ZA, X, Y, X | Y)]
    weights, token = fetch((w_gate[0], w_up[0], w_down[0]), start[1])
    near, zs, ps = combine(
        [[0, ZA, X, Y, ZB, X | Y], [ZA, ZB], [X | Y, ZB]], [start, za, x, y, zb, xy], rows, [token]
    )

    near, xs, ys, pz, xyb = sums(
        [near], send(X, zs), send(Y, zs), send(ZA, ps), send(X | Y, zb)
    )
    side, rest, zab = combine(
        [[X | ZA, X | ZB, Y | ZA, Y | ZB, X | Y | ZA], [ZA | ZB, X | Y | ZB], [ZA | ZB]],
        [xs, ys, pz, xyb],
        rows,
    )
    side, *got = sums([side], send(X, zab), send(Y, zab), send(ZA, xyb))
    (far,) = combine([[X | ZA | ZB, Y | ZA | ZB, X | Y | ZA | ZB]], got, rows)
    x, y, xya = combine([[X | ZA, X | ZB], [Y | ZA, Y | ZB], [X | Y | ZA]], side, rows)
    far, x, y, xya = sums([rest, far], send(X, x), send(Y, y), send(ZA, xya))

    xa, ya, xyab = combine([[X | ZA | ZB], [Y | ZA | ZB], [X | Y | ZA | ZB]], far, rows)
    got = send(X, xa), send(Y, ya), send(ZA, xyab)
    zab, xyb = combine([[ZA | ZB], [X | Y | ZB]], [*far, *got], rows)
    got = x, y, xya, send(ZA, zab), send(X | Y, xyb)
    ends = combine([[ZB], [X], [Y], [ZA], [X | Y]], [*near, *got], rows)
    return combine([[0]], [*near, *(send(piece[0][0], piece) for piece in ends)], rows)[0][1]


def dispatch(hidden_in, routes, scores, w_gate, w_up, w_down):
    rows_dev, model_width = hidden_in.shape
    top_k = routes.shape[1]
    experts = lax.axis_size("dev")
    slots_dev = 2 * rows_dev * top_k // experts
    slot_rows = experts * slots_dev
    normed = normalise(hidden_in)
    shares = scores / jnp.sum(scores, -1, keepdims=True)
    chosen = routes.reshape(-1)
    onehot = (chosen[:, None] == jnp.arange(experts, dtype=jnp.int32)[None, :]).astype(jnp.int32)
    before = jnp.cumsum(onehot, 0) - onehot
    position = jnp.sum(before * onehot, 1)
    target = (chosen * slots_dev + position).reshape(rows_dev, top_k)
    places = jnp.arange(slot_rows, dtype=jnp.int32)
    picker = jnp.any(target[None, :, :] == places[:, None, None], -1).astype(jnp.bfloat16)
    outgoing = jnp.dot(picker, normed, preferred_element_type=jnp.float32).astype(jnp.bfloat16)
    outgoing = outgoing.reshape(experts, slots_dev, model_width)
    arrived = lax.all_to_all(outgoing, "dev", split_axis=0, concat_axis=0, tiled=True).reshape(
        slot_rows, model_width
    )
    paired = lax.all_gather(arrived, "sec", axis=0, tiled=True)
    result = lax.psum_scatter(
        expert(paired, w_gate[0], w_up[0], w_down[0]).astype(jnp.bfloat16),
        "sec",
        scatter_dimension=0,
        tiled=True,
    )
    expert_out = result.reshape(experts, slots_dev, model_width)
    returned = lax.all_to_all(expert_out, "dev", split_axis=0, concat_axis=0, tiled=True).reshape(
        slot_rows, model_width
    )
    picked = jnp.take(returned, target.reshape(-1), axis=0).reshape(rows_dev, top_k, model_width)
    combined = jnp.einsum("rk,rkd->rd", shares, picked.astype(jnp.float32))
    return combined.astype(jnp.bfloat16)


def on_device(hidden_in, routes, scores, *weights):
    experts, halves = lax.axis_size("dev"), lax.axis_size("sec")
    roomy = 2 * routes.shape[1] >= experts
    plan = spread if roomy and (halves, experts) == (2, 16) else dispatch
    return plan(hidden_in, routes, scores, *weights)


def solution(mesh):
    placed = (
        P(("sec", "dev"), None),
        P(("sec", "dev"), None),
        P(("sec", "dev"), None),
        P("dev", None, "sec"),
        P("dev", None, "sec"),
        P("dev", "sec", None),
    )
    return jax.shard_map(
        on_device, mesh=mesh, in_specs=placed, out_specs=P(("sec", "dev"), None), check_vma=False
    )
```

```python
import functools

import jax
import jax.numpy as jnp
from jax import lax
from jax.experimental import pallas as pl
from jax.experimental.pallas import tpu as pltpu
from jax.sharding import PartitionSpec as P

BOTH = ("sec", "dev")
CORE, X, ZA, ZB, Y = 1, 2, 4, 8, 16
TERMS = 3
VMEM = pl.BlockSpec(memory_space=pltpu.VMEM)


def normalise(hidden_in):
    values = hidden_in.astype(jnp.float32)
    return (values * lax.rsqrt(jnp.mean(values * values, -1, keepdims=True) + 1e-06)).astype(
        jnp.bfloat16
    )


def swap(block, mask, devices):
    return lax.ppermute(block, BOTH, [(i, i ^ mask) for i in range(devices)])


def expert(rows, w_gate, w_up, w_down):
    gate_part = jnp.dot(rows, w_gate, preferred_element_type=jnp.float32)
    up_part = jnp.dot(rows, w_up, preferred_element_type=jnp.float32)
    hidden_part = (jax.nn.silu(gate_part) * up_part).astype(jnp.bfloat16)
    return jnp.dot(hidden_part, w_down, preferred_element_type=jnp.float32)


def local(body, outs, operands, scratch=(), limit=12, after=(), **cost):
    return pl.pallas_call(
        body,
        out_shape=[jax.ShapeDtypeStruct(shape, jnp.bfloat16) for shape in outs],
        in_specs=[VMEM] * len(operands) + [pl.BlockSpec(memory_space=pl.ANY)] * len(after),
        out_specs=[VMEM] * len(outs),
        scratch_shapes=list(scratch),
        compiler_params=pltpu.CompilerParams(vmem_limit_bytes=limit * 2**20),
        cost_estimate=pl.CostEstimate(**{"flops": 0, "transcendentals": 0, "bytes_accessed": 0, **cost}),
    )(*operands, *after)


def prepare_body(experts, *refs):
    count = 3
    sources, (_, out_ref), (held, sems) = refs[:count], refs[count : count + 2], (refs[count + 2 : -1], refs[-1])
    copies = [pltpu.make_async_copy(sources[at], held[at], sems.at[at]) for at in range(count)]
    for copy in copies:
        copy.start()
    for copy in copies:
        copy.wait()
    hidden_ref, routes_ref, scores_ref = held
    width = hidden_ref.shape[1]
    out_ref[:, :width] = normalise(hidden_ref[...])
    scores = scores_ref[...]
    shares = scores / jnp.sum(scores, 0, keepdims=True)
    lanes = lax.broadcasted_iota(jnp.int32, (128, hidden_ref.shape[0]), 0)
    table = jnp.zeros(lanes.shape, jnp.float32)
    for k in range(routes_ref.shape[0]):
        named = routes_ref[k : k + 1, :] == lanes % experts
        table = table + jnp.where(named, shares[k : k + 1, :], 0.0)
    packed = jnp.zeros(lanes.shape, jnp.float32)
    for at in range(TERMS):
        term = table.astype(jnp.bfloat16).astype(jnp.float32)
        packed = jnp.where(lanes // experts == at, term, packed)
        table = table - term
    out_ref[:, width:] = packed.T.astype(jnp.bfloat16)


def prepare(hidden_in, routes, scores, experts, after):
    rows, width = hidden_in.shape
    arrays = hidden_in, routes.T, scores.T
    anywhere = pl.BlockSpec(memory_space=pl.ANY)
    return pl.pallas_call(
        functools.partial(prepare_body, experts),
        out_shape=jax.ShapeDtypeStruct((rows, width + 128), jnp.bfloat16),
        in_specs=[anywhere] * 4,
        out_specs=VMEM,
        scratch_shapes=[
            *(pltpu.VMEM(a.shape, a.dtype) for a in arrays),
            pltpu.SemaphoreType.DMA((len(arrays),)),
        ],
        compiler_params=pltpu.CompilerParams(vmem_limit_bytes=4 * 2**20),
    )(*(pltpu.with_memory_space_constraint(a, pltpu.HBM) for a in arrays), after)


def fetch_body(count, after_ref, *refs):
    sources, outs, (token_ref, sems) = refs[:count], refs[count : 2 * count], refs[2 * count :]
    token_ref[...] = jnp.zeros(token_ref.shape, token_ref.dtype)
    copies = [pltpu.make_async_copy(sources[at], outs[at], sems.at[at]) for at in range(count)]
    for copy in copies:
        copy.start()
    for copy in copies:
        copy.wait()


def fetch(arrays, after):
    sources = [pltpu.with_memory_space_constraint(a, pltpu.HBM) for a in arrays]
    anywhere = pl.BlockSpec(memory_space=pl.ANY)
    *outs, token = pl.pallas_call(
        functools.partial(fetch_body, len(arrays)),
        out_shape=[pltpu.VMEM(a.shape, a.dtype) for a in arrays]
        + [jax.ShapeDtypeStruct((16, 128), jnp.bfloat16)],
        in_specs=[anywhere] * (1 + len(arrays)),
        out_specs=[VMEM] * (len(arrays) + 1),
        scratch_shapes=[pltpu.SemaphoreType.DMA((len(arrays),))],
        compiler_params=pltpu.CompilerParams(vmem_limit_bytes=4 * 2**20),
    )(after, *sources)
    return [pltpu.with_memory_space_constraint(a, pltpu.VMEM) for a in outs], token


def expert_body(count, mine_ref, *refs):
    blocks, (gate_ref, up_ref, down_ref) = refs[:count], refs[count : count + 3]
    own_ref, *other_refs, rows_ref, hidden_ref = refs[count + 3 :]
    width, first = down_ref.shape[1], 0
    shares = []
    for block in blocks:
        rows_ref[first : first + block.shape[0], :] = block[:, :width]
        first += block.shape[0]
        shares.append(jnp.sum(block[:, width:].astype(jnp.float32) * mine_ref[...], -1, keepdims=True))
    weight = jnp.concatenate(shares, 0)
    for at in range(0, gate_ref.shape[1], 256):
        cols = slice(at, at + 256)
        gate_part = jnp.dot(rows_ref[...], gate_ref[:, cols], preferred_element_type=jnp.float32)
        up_part = jnp.dot(rows_ref[...], up_ref[:, cols], preferred_element_type=jnp.float32)
        hidden_ref[:, cols] = (gate_part / (1.0 + jnp.exp(-gate_part)) * up_part).astype(jnp.bfloat16)
    half = first // 2

    for start in range(0, width, 1024):
        cols = slice(start, start + 1024)
        out = jnp.dot(hidden_ref[...], down_ref[:, cols], preferred_element_type=jnp.float32) * weight
        own_ref[:, cols] = out[:half].astype(jnp.bfloat16)
        at = half
        for other_ref in other_refs:
            other_ref[:, cols] = out[at : at + other_ref.shape[0]].astype(jnp.bfloat16)
            at += other_ref.shape[0]


def expert_rows(blocks, mine, w_gate, w_up, w_down, cuts):
    rows = sum(block.shape[0] for block in blocks)
    width, units = w_down.shape[1], w_gate.shape[1]
    return local(
        functools.partial(expert_body, len(blocks)),
        [(rows // 2, width), *((cut, width) for cut in cuts)],
        (mine, *blocks, w_gate, w_up, w_down),
        [pltpu.VMEM((rows, width), jnp.bfloat16), pltpu.VMEM((rows, units), jnp.bfloat16)],
        flops=6 * rows * width * units,
        bytes_accessed=2 * rows * width,
    )


def add_body(plan, count, rows, *refs):
    for out, blocks in zip(refs[count:], plan):
        for at, parts in enumerate(blocks):
            cut = [refs[ref][place * rows : (place + 1) * rows, :] for ref, place in parts]
            if len(cut) > 1:
                cut = [sum(part.astype(jnp.float32) for part in cut).astype(jnp.bfloat16)]
            out[at * rows : (at + 1) * rows, :] = cut[0]


def combine(wanted, pieces, rows, after=()):
    plan = [
        [
            [(ref, names.index(m)) for ref, (names, _) in enumerate(pieces) if m in names]
            for m in blocks
        ]
        for blocks in wanted
    ]
    arrays = [array for _, array in pieces]
    width = arrays[0].shape[1]
    outs = local(
        functools.partial(add_body, plan, len(arrays) + len(after), rows),
        [(len(blocks) * rows, width) for blocks in wanted],
        arrays,
        limit=4,
        after=after,
    )
    return list(zip(wanted, outs))


def spread(hidden_in, routes, scores, w_gate, w_up, w_down):
    rows = hidden_in.shape[0]
    experts = lax.axis_size("dev")
    devices = experts * lax.axis_size("sec")
    lanes = jnp.arange(128)
    mine = (lanes % experts == lax.axis_index("dev")) & (lanes < TERMS * experts)
    mine = mine.astype(jnp.float32)[None, :]

    def send(link, piece):
        names, array = piece
        return tuple(m ^ link for m in names), swap(array, link, devices)

    def shares(pieces, *cuts):
        names = sum((tuple(names) for names, _ in pieces), ())
        here = [array for _, array in pieces]
        there = [swap(array, CORE, devices) for array in here]
        cuts = cuts or (len(names),)
        own, *others = expert_rows(here + there, mine, *weights, [cut * rows for cut in cuts])
        starts = [sum(cuts[:at]) for at in range(len(cuts))]
        parts = [tuple(m ^ CORE for m in names[at : at + cut]) for at, cut in zip(starts, cuts)]
        return [(names, own), *zip(parts, others)]

    def tie(*pieces):
        arrays = lax.optimization_barrier(tuple(array for _, array in pieces))
        return [(names, array) for (names, _), array in zip(pieces, arrays)]

    def sums(pieces, *beside):
        own, other, *beside = tie(*shares(pieces), *beside)
        return [own, send(CORE, other)], *beside

    start = [0], prepare(hidden_in, routes, scores, experts, mine)
    zb, x, y, xy, za = [send(link, start) for link in (ZB, X, Y, X | Y, ZA)]
    weights, token = fetch((w_gate[0], w_up[0], w_down[0]), start[1])
    near, zs, ps = combine(
        [[0, ZA, X, Y, ZB, X | Y], [ZA, ZB], [X | Y, ZB]], [zb, x, y, xy, za, start], rows, [token]
    )

    near, xs, ys, pz, xyb = sums(
        [near], send(X, zs), send(Y, zs), send(ZA, ps), send(X | Y, zb)
    )
    side, rest, zab = combine(
        [[X | ZA, X | ZB, Y | ZA, Y | ZB, X | Y | ZA], [ZA | ZB, X | Y | ZB], [ZA | ZB]],
        [xs, ys, pz, xyb],
        rows,
    )
    side, *got = sums([side], send(X, zab), send(Y, zab), send(ZA, xyb))
    (far,) = combine([[X | ZA | ZB, Y | ZA | ZB, X | Y | ZA | ZB]], got, rows)
    x, y, xya = combine([[X | ZA, X | ZB], [Y | ZA, Y | ZB], [X | Y | ZA]], side, rows)
    own, *others = shares([far, rest], 1, 2, 2)
    own, x, y, xya = tie(own, send(X, x), send(Y, y), send(ZA, xya))
    far = [own, *(send(CORE, other) for other in others)]
    (x,) = combine([[ZA, ZB]], [x, y], rows)

    xa, ya, xyab = combine(
        [[X | ZA | ZB], [Y | ZA | ZB], [X | Y | ZA | ZB]], far, rows, [x[1]]
    )
    got = send(X, xa), send(Y, ya), send(ZA, xyab)
    zab, xyb = combine([[ZA | ZB], [X | Y | ZB]], [*far, *got], rows)
    got = x, xya, send(ZA, zab), send(X | Y, xyb)
    ends = combine([[ZB], [X], [Y], [ZA], [X | Y]], [*near, *got], rows)
    ends = [send(piece[0][0], piece) for piece in ends]
    return combine([[0]], [*ends, *near], rows)[0][1]


def dispatch(hidden_in, routes, scores, w_gate, w_up, w_down):
    rows_dev, model_width = hidden_in.shape
    top_k = routes.shape[1]
    experts = lax.axis_size("dev")
    slots_dev = 2 * rows_dev * top_k // experts
    slot_rows = experts * slots_dev
    normed = normalise(hidden_in)
    shares = scores / jnp.sum(scores, -1, keepdims=True)
    chosen = routes.reshape(-1)
    onehot = (chosen[:, None] == jnp.arange(experts, dtype=jnp.int32)[None, :]).astype(jnp.int32)
    before = jnp.cumsum(onehot, 0) - onehot
    position = jnp.sum(before * onehot, 1)
    target = (chosen * slots_dev + position).reshape(rows_dev, top_k)
    places = jnp.arange(slot_rows, dtype=jnp.int32)
    picker = jnp.any(target[None, :, :] == places[:, None, None], -1).astype(jnp.bfloat16)
    outgoing = jnp.dot(picker, normed, preferred_element_type=jnp.float32).astype(jnp.bfloat16)
    outgoing = outgoing.reshape(experts, slots_dev, model_width)
    arrived = lax.all_to_all(outgoing, "dev", split_axis=0, concat_axis=0, tiled=True).reshape(
        slot_rows, model_width
    )
    paired = lax.all_gather(arrived, "sec", axis=0, tiled=True)
    result = lax.psum_scatter(
        expert(paired, w_gate[0], w_up[0], w_down[0]).astype(jnp.bfloat16),
        "sec",
        scatter_dimension=0,
        tiled=True,
    )
    expert_out = result.reshape(experts, slots_dev, model_width)
    returned = lax.all_to_all(expert_out, "dev", split_axis=0, concat_axis=0, tiled=True).reshape(
        slot_rows, model_width
    )
    picked = jnp.take(returned, target.reshape(-1), axis=0).reshape(rows_dev, top_k, model_width)
    combined = jnp.einsum("rk,rkd->rd", shares, picked.astype(jnp.float32))
    return combined.astype(jnp.bfloat16)


def on_device(hidden_in, routes, scores, *weights):
    experts, halves = lax.axis_size("dev"), lax.axis_size("sec")
    roomy = 2 * routes.shape[1] >= experts
    plan = spread if roomy and (halves, experts) == (2, 16) else dispatch
    return plan(hidden_in, routes, scores, *weights)


def solution(mesh):
    placed = (
        P(("sec", "dev"), None),
        P(("sec", "dev"), None),
        P(("sec", "dev"), None),
        P("dev", None, "sec"),
        P("dev", None, "sec"),
        P("dev", "sec", None),
    )
    return jax.shard_map(
        on_device, mesh=mesh, in_specs=placed, out_specs=P(("sec", "dev"), None), check_vma=False
    )
```

```python
import functools

import jax
import jax.numpy as jnp
from jax import lax
from jax.experimental import pallas as pl
from jax.experimental.pallas import tpu as pltpu
from jax.sharding import PartitionSpec as P

BOTH = ("sec", "dev")
CORE, X, ZA, ZB, Y = 1, 2, 4, 8, 16
TERMS = 3
VMEM = pl.BlockSpec(memory_space=pltpu.VMEM)


def normalise(hidden_in):
    values = hidden_in.astype(jnp.float32)
    return (values * lax.rsqrt(jnp.mean(values * values, -1, keepdims=True) + 1e-06)).astype(
        jnp.bfloat16
    )


def swap(block, mask, devices):
    return lax.ppermute(block, BOTH, [(i, i ^ mask) for i in range(devices)])


def expert(rows, w_gate, w_up, w_down):
    gate_part = jnp.dot(rows, w_gate, preferred_element_type=jnp.float32)
    up_part = jnp.dot(rows, w_up, preferred_element_type=jnp.float32)
    hidden_part = (jax.nn.silu(gate_part) * up_part).astype(jnp.bfloat16)
    return jnp.dot(hidden_part, w_down, preferred_element_type=jnp.float32)


def local(body, outs, operands, scratch=(), limit=12, after=(), **cost):
    return pl.pallas_call(
        body,
        out_shape=[jax.ShapeDtypeStruct(shape, jnp.bfloat16) for shape in outs],
        in_specs=[VMEM] * len(operands) + [pl.BlockSpec(memory_space=pl.ANY)] * len(after),
        out_specs=[VMEM] * len(outs),
        scratch_shapes=list(scratch),
        compiler_params=pltpu.CompilerParams(vmem_limit_bytes=limit * 2**20),
        cost_estimate=pl.CostEstimate(**{"flops": 0, "transcendentals": 0, "bytes_accessed": 0, **cost}),
    )(*operands, *after)


def prepare_body(experts, *refs):
    count = 3
    sources, (_, out_ref), (held, sems) = refs[:count], refs[count : count + 2], (refs[count + 2 : -1], refs[-1])
    copies = [pltpu.make_async_copy(sources[at], held[at], sems.at[at]) for at in range(count)]
    for copy in copies:
        copy.start()
    for copy in copies:
        copy.wait()
    hidden_ref, routes_ref, scores_ref = held
    width = hidden_ref.shape[1]
    out_ref[:, :width] = normalise(hidden_ref[...])
    scores = scores_ref[...]
    shares = scores / jnp.sum(scores, 0, keepdims=True)
    lanes = lax.broadcasted_iota(jnp.int32, (128, hidden_ref.shape[0]), 0)
    table = jnp.zeros(lanes.shape, jnp.float32)
    for k in range(routes_ref.shape[0]):
        named = routes_ref[k : k + 1, :] == lanes % experts
        table = table + jnp.where(named, shares[k : k + 1, :], 0.0)
    packed = jnp.zeros(lanes.shape, jnp.float32)
    for at in range(TERMS):
        term = table.astype(jnp.bfloat16).astype(jnp.float32)
        packed = jnp.where(lanes // experts == at, term, packed)
        table = table - term
    out_ref[:, width:] = packed.T.astype(jnp.bfloat16)


def prepare(hidden_in, routes, scores, experts, after):
    rows, width = hidden_in.shape
    arrays = hidden_in, routes.T, scores.T
    anywhere = pl.BlockSpec(memory_space=pl.ANY)
    return pl.pallas_call(
        functools.partial(prepare_body, experts),
        out_shape=jax.ShapeDtypeStruct((rows, width + 128), jnp.bfloat16),
        in_specs=[anywhere] * 4,
        out_specs=VMEM,
        scratch_shapes=[
            *(pltpu.VMEM(a.shape, a.dtype) for a in arrays),
            pltpu.SemaphoreType.DMA((len(arrays),)),
        ],
        compiler_params=pltpu.CompilerParams(vmem_limit_bytes=4 * 2**20),
    )(*(pltpu.with_memory_space_constraint(a, pltpu.HBM) for a in arrays), after)


def fetch_body(count, after_ref, *refs):
    sources, outs, (token_ref, sems) = refs[:count], refs[count : 2 * count], refs[2 * count :]
    token_ref[...] = jnp.zeros(token_ref.shape, token_ref.dtype)
    copies = [pltpu.make_async_copy(sources[at], outs[at], sems.at[at]) for at in range(count)]
    for copy in copies:
        copy.start()
    for copy in copies:
        copy.wait()


def fetch(arrays, after):
    sources = [pltpu.with_memory_space_constraint(a, pltpu.HBM) for a in arrays]
    anywhere = pl.BlockSpec(memory_space=pl.ANY)
    *outs, token = pl.pallas_call(
        functools.partial(fetch_body, len(arrays)),
        out_shape=[pltpu.VMEM(a.shape, a.dtype) for a in arrays]
        + [jax.ShapeDtypeStruct((16, 128), jnp.bfloat16)],
        in_specs=[anywhere] * (1 + len(arrays)),
        out_specs=[VMEM] * (len(arrays) + 1),
        scratch_shapes=[pltpu.SemaphoreType.DMA((len(arrays),))],
        compiler_params=pltpu.CompilerParams(vmem_limit_bytes=4 * 2**20),
    )(after, *sources)
    return [pltpu.with_memory_space_constraint(a, pltpu.VMEM) for a in outs], token


def expert_body(count, mine_ref, *refs):
    blocks, (gate_ref, up_ref, down_ref) = refs[:count], refs[count : count + 3]
    own_ref, *other_refs, rows_ref, hidden_ref = refs[count + 3 :]
    width, first = down_ref.shape[1], 0
    shares = []
    for block in blocks:
        rows_ref[first : first + block.shape[0], :] = block[:, :width]
        first += block.shape[0]
        shares.append(jnp.sum(block[:, width:].astype(jnp.float32) * mine_ref[...], -1, keepdims=True))
    weight = jnp.concatenate(shares, 0)
    for at in range(0, gate_ref.shape[1], 256):
        cols = slice(at, at + 256)
        gate_part = jnp.dot(rows_ref[...], gate_ref[:, cols], preferred_element_type=jnp.float32)
        up_part = jnp.dot(rows_ref[...], up_ref[:, cols], preferred_element_type=jnp.float32)
        hidden_ref[:, cols] = (gate_part / (1.0 + jnp.exp(-gate_part)) * up_part).astype(jnp.bfloat16)
    half = first // 2

    for start in range(0, width, 1024):
        cols = slice(start, start + 1024)
        out = jnp.dot(hidden_ref[...], down_ref[:, cols], preferred_element_type=jnp.float32) * weight
        own_ref[:, cols] = out[:half].astype(jnp.bfloat16)
        at = half
        for other_ref in other_refs:
            other_ref[:, cols] = out[at : at + other_ref.shape[0]].astype(jnp.bfloat16)
            at += other_ref.shape[0]


def expert_rows(blocks, mine, w_gate, w_up, w_down, cuts):
    rows = sum(block.shape[0] for block in blocks)
    width, units = w_down.shape[1], w_gate.shape[1]
    return local(
        functools.partial(expert_body, len(blocks)),
        [(rows // 2, width), *((cut, width) for cut in cuts)],
        (mine, *blocks, w_gate, w_up, w_down),
        [pltpu.VMEM((rows, width), jnp.bfloat16), pltpu.VMEM((rows, units), jnp.bfloat16)],
        flops=6 * rows * width * units,
        bytes_accessed=2 * rows * width,
    )


def add_body(plan, count, rows, *refs):
    for out, blocks in zip(refs[count:], plan):
        for at, parts in enumerate(blocks):
            cut = [refs[ref][place * rows : (place + 1) * rows, :] for ref, place in parts]
            if len(cut) > 1:
                cut = [sum(part.astype(jnp.float32) for part in cut).astype(jnp.bfloat16)]
            out[at * rows : (at + 1) * rows, :] = cut[0]


def combine(wanted, pieces, rows, after=()):
    plan = [
        [
            [(ref, names.index(m)) for ref, (names, _) in enumerate(pieces) if m in names]
            for m in blocks
        ]
        for blocks in wanted
    ]
    arrays = [array for _, array in pieces]
    width = arrays[0].shape[1]
    outs = local(
        functools.partial(add_body, plan, len(arrays) + len(after), rows),
        [(len(blocks) * rows, width) for blocks in wanted],
        arrays,
        limit=4,
        after=after,
    )
    return list(zip(wanted, outs))


def spread(hidden_in, routes, scores, w_gate, w_up, w_down):
    rows = hidden_in.shape[0]
    experts = lax.axis_size("dev")
    devices = experts * lax.axis_size("sec")
    lanes = jnp.arange(128)
    mine = (lanes % experts == lax.axis_index("dev")) & (lanes < TERMS * experts)
    mine = mine.astype(jnp.float32)[None, :]

    def send(link, piece):
        names, array = piece
        return tuple(m ^ link for m in names), swap(array, link, devices)

    def shares(pieces, *cuts):
        names = sum((tuple(names) for names, _ in pieces), ())
        here = [array for _, array in pieces]
        there = [swap(array, CORE, devices) for array in here]
        cuts = cuts or (len(names),)
        own, *others = expert_rows(here + there, mine, *weights, [cut * rows for cut in cuts])
        starts = [sum(cuts[:at]) for at in range(len(cuts))]
        parts = [tuple(m ^ CORE for m in names[at : at + cut]) for at, cut in zip(starts, cuts)]
        return [(names, own), *zip(parts, others)]

    def tie(*pieces):
        arrays = lax.optimization_barrier(tuple(array for _, array in pieces))
        return [(names, array) for (names, _), array in zip(pieces, arrays)]

    def sums(pieces, *beside):
        own, other, *beside = tie(*shares(pieces), *beside)
        return [own, send(CORE, other)], *beside

    start = [0], prepare(hidden_in, routes, scores, experts, mine)
    zb, x, y, xy, za = [send(link, start) for link in (ZB, X, Y, X | Y, ZA)]
    weights, token = fetch((w_gate[0], w_up[0], w_down[0]), start[1])
    near, zs, ps = combine(
        [[0, ZA, X, Y, ZB, X | Y], [ZA, ZB], [X | Y, ZB]], [start, za, x, y, zb, xy], rows, [token]
    )

    near, xs, ys, pz, xyb = sums(
        [near], send(X, zs), send(Y, zs), send(ZA, ps), send(X | Y, zb)
    )
    side, rest, zab = combine(
        [[X | ZA, X | ZB, Y | ZA, Y | ZB, X | Y | ZA], [ZA | ZB, X | Y | ZB], [ZA | ZB]],
        [xs, ys, pz, xyb],
        rows,
    )
    side, *got = sums([side], send(X, zab), send(Y, zab), send(ZA, xyb))
    (far,) = combine([[X | ZA | ZB, Y | ZA | ZB, X | Y | ZA | ZB]], got, rows)
    x, y, xya = combine([[X | ZA, X | ZB], [Y | ZA, Y | ZB], [X | Y | ZA]], side, rows)
    own, *others = shares([far, rest], 1, 2, 2)
    own, x, y, xya = tie(own, send(X, x), send(Y, y), send(ZA, xya))
    far = [own, *(send(CORE, other) for other in others)]
    (x,) = combine([[ZA, ZB]], [x, y], rows)

    xyab, xa, ya = combine(
        [[X | Y | ZA | ZB], [X | ZA | ZB], [Y | ZA | ZB]], far, rows, [x[1]]
    )
    xyab, xa, ya = send(ZA, xyab), send(X, xa), send(Y, ya)
    (xyb,) = combine([[X | Y | ZB]], [*far, xyab], rows)
    xyb = send(X | Y, xyb)
    (zab,) = combine([[ZA | ZB]], [*far, xa, ya], rows)
    got = x, xya, xyb, send(ZA, zab)
    ends = combine([[ZB], [X], [Y], [ZA], [X | Y]], [*near, *got], rows)
    ends = [send(piece[0][0], piece) for piece in ends]
    return combine([[0]], [*ends, *near], rows)[0][1]


def dispatch(hidden_in, routes, scores, w_gate, w_up, w_down):
    rows_dev, model_width = hidden_in.shape
    top_k = routes.shape[1]
    experts = lax.axis_size("dev")
    slots_dev = 2 * rows_dev * top_k // experts
    slot_rows = experts * slots_dev
    normed = normalise(hidden_in)
    shares = scores / jnp.sum(scores, -1, keepdims=True)
    chosen = routes.reshape(-1)
    onehot = (chosen[:, None] == jnp.arange(experts, dtype=jnp.int32)[None, :]).astype(jnp.int32)
    before = jnp.cumsum(onehot, 0) - onehot
    position = jnp.sum(before * onehot, 1)
    target = (chosen * slots_dev + position).reshape(rows_dev, top_k)
    places = jnp.arange(slot_rows, dtype=jnp.int32)
    picker = jnp.any(target[None, :, :] == places[:, None, None], -1).astype(jnp.bfloat16)
    outgoing = jnp.dot(picker, normed, preferred_element_type=jnp.float32).astype(jnp.bfloat16)
    outgoing = outgoing.reshape(experts, slots_dev, model_width)
    arrived = lax.all_to_all(outgoing, "dev", split_axis=0, concat_axis=0, tiled=True).reshape(
        slot_rows, model_width
    )
    paired = lax.all_gather(arrived, "sec", axis=0, tiled=True)
    result = lax.psum_scatter(
        expert(paired, w_gate[0], w_up[0], w_down[0]).astype(jnp.bfloat16),
        "sec",
        scatter_dimension=0,
        tiled=True,
    )
    expert_out = result.reshape(experts, slots_dev, model_width)
    returned = lax.all_to_all(expert_out, "dev", split_axis=0, concat_axis=0, tiled=True).reshape(
        slot_rows, model_width
    )
    picked = jnp.take(returned, target.reshape(-1), axis=0).reshape(rows_dev, top_k, model_width)
    combined = jnp.einsum("rk,rkd->rd", shares, picked.astype(jnp.float32))
    return combined.astype(jnp.bfloat16)


def on_device(hidden_in, routes, scores, *weights):
    experts, halves = lax.axis_size("dev"), lax.axis_size("sec")
    roomy = 2 * routes.shape[1] >= experts
    plan = spread if roomy and (halves, experts) == (2, 16) else dispatch
    return plan(hidden_in, routes, scores, *weights)


def solution(mesh):
    placed = (
        P(("sec", "dev"), None),
        P(("sec", "dev"), None),
        P(("sec", "dev"), None),
        P("dev", None, "sec"),
        P("dev", None, "sec"),
        P("dev", "sec", None),
    )
    return jax.shard_map(
        on_device, mesh=mesh, in_specs=placed, out_specs=P(("sec", "dev"), None), check_vma=False
    )
```

```python
import functools

import jax
import jax.numpy as jnp
from jax import lax
from jax.experimental import pallas as pl
from jax.experimental.pallas import tpu as pltpu
from jax.sharding import PartitionSpec as P

BOTH = ("sec", "dev")
CORE, X, ZA, ZB, Y = 1, 2, 4, 8, 16
TERMS = 3
VMEM = pl.BlockSpec(memory_space=pltpu.VMEM)


def normalise(hidden_in):
    values = hidden_in.astype(jnp.float32)
    return (values * lax.rsqrt(jnp.mean(values * values, -1, keepdims=True) + 1e-06)).astype(
        jnp.bfloat16
    )


def swap(block, mask, devices):
    return lax.ppermute(block, BOTH, [(i, i ^ mask) for i in range(devices)])


def expert(rows, w_gate, w_up, w_down):
    gate_part = jnp.dot(rows, w_gate, preferred_element_type=jnp.float32)
    up_part = jnp.dot(rows, w_up, preferred_element_type=jnp.float32)
    hidden_part = (jax.nn.silu(gate_part) * up_part).astype(jnp.bfloat16)
    return jnp.dot(hidden_part, w_down, preferred_element_type=jnp.float32)


def local(body, outs, operands, scratch=(), limit=12, after=(), **cost):
    return pl.pallas_call(
        body,
        out_shape=[jax.ShapeDtypeStruct(shape, jnp.bfloat16) for shape in outs],
        in_specs=[VMEM] * len(operands) + [pl.BlockSpec(memory_space=pl.ANY)] * len(after),
        out_specs=[VMEM] * len(outs),
        scratch_shapes=list(scratch),
        compiler_params=pltpu.CompilerParams(vmem_limit_bytes=limit * 2**20),
        cost_estimate=pl.CostEstimate(**{"flops": 0, "transcendentals": 0, "bytes_accessed": 0, **cost}),
    )(*operands, *after)


def prepare_body(experts, *refs):
    count = 3
    sources, (_, out_ref), (held, sems) = refs[:count], refs[count : count + 2], (refs[count + 2 : -1], refs[-1])
    copies = [pltpu.make_async_copy(sources[at], held[at], sems.at[at]) for at in range(count)]
    for copy in copies:
        copy.start()
    for copy in copies:
        copy.wait()
    hidden_ref, routes_ref, scores_ref = held
    width = hidden_ref.shape[1]
    out_ref[:, :width] = normalise(hidden_ref[...])
    scores = scores_ref[...]
    shares = scores / jnp.sum(scores, 0, keepdims=True)
    lanes = lax.broadcasted_iota(jnp.int32, (128, hidden_ref.shape[0]), 0)
    table = jnp.zeros(lanes.shape, jnp.float32)
    for k in range(routes_ref.shape[0]):
        named = routes_ref[k : k + 1, :] == lanes % experts
        table = table + jnp.where(named, shares[k : k + 1, :], 0.0)
    packed = jnp.zeros(lanes.shape, jnp.float32)
    for at in range(TERMS):
        term = table.astype(jnp.bfloat16).astype(jnp.float32)
        packed = jnp.where(lanes // experts == at, term, packed)
        table = table - term
    out_ref[:, width:] = packed.T.astype(jnp.bfloat16)


def prepare(hidden_in, routes, scores, experts, after):
    rows, width = hidden_in.shape
    arrays = hidden_in, routes.T, scores.T
    anywhere = pl.BlockSpec(memory_space=pl.ANY)
    return pl.pallas_call(
        functools.partial(prepare_body, experts),
        out_shape=jax.ShapeDtypeStruct((rows, width + 128), jnp.bfloat16),
        in_specs=[anywhere] * 4,
        out_specs=VMEM,
        scratch_shapes=[
            *(pltpu.VMEM(a.shape, a.dtype) for a in arrays),
            pltpu.SemaphoreType.DMA((len(arrays),)),
        ],
        compiler_params=pltpu.CompilerParams(vmem_limit_bytes=4 * 2**20),
    )(*(pltpu.with_memory_space_constraint(a, pltpu.HBM) for a in arrays), after)


def fetch_body(count, after_ref, *refs):
    sources, outs, (token_ref, sems) = refs[:count], refs[count : 2 * count], refs[2 * count :]
    token_ref[...] = jnp.zeros(token_ref.shape, token_ref.dtype)
    copies = [pltpu.make_async_copy(sources[at], outs[at], sems.at[at]) for at in range(count)]
    for copy in copies:
        copy.start()
    for copy in copies:
        copy.wait()


def fetch(arrays, after):
    sources = [pltpu.with_memory_space_constraint(a, pltpu.HBM) for a in arrays]
    anywhere = pl.BlockSpec(memory_space=pl.ANY)
    *outs, token = pl.pallas_call(
        functools.partial(fetch_body, len(arrays)),
        out_shape=[pltpu.VMEM(a.shape, a.dtype) for a in arrays]
        + [jax.ShapeDtypeStruct((16, 128), jnp.bfloat16)],
        in_specs=[anywhere] * (1 + len(arrays)),
        out_specs=[VMEM] * (len(arrays) + 1),
        scratch_shapes=[pltpu.SemaphoreType.DMA((len(arrays),))],
        compiler_params=pltpu.CompilerParams(vmem_limit_bytes=4 * 2**20),
    )(after, *sources)
    return [pltpu.with_memory_space_constraint(a, pltpu.VMEM) for a in outs], token


def expert_body(count, mine_ref, *refs):
    blocks, (gate_ref, up_ref, down_ref) = refs[:count], refs[count : count + 3]
    own_ref, *other_refs, rows_ref, hidden_ref = refs[count + 3 :]
    width, first = down_ref.shape[1], 0
    shares = []
    for block in blocks:
        rows_ref[first : first + block.shape[0], :] = block[:, :width]
        first += block.shape[0]
        shares.append(jnp.sum(block[:, width:].astype(jnp.float32) * mine_ref[...], -1, keepdims=True))
    weight = jnp.concatenate(shares, 0)
    for at in range(0, gate_ref.shape[1], 256):
        cols = slice(at, at + 256)
        gate_part = jnp.dot(rows_ref[...], gate_ref[:, cols], preferred_element_type=jnp.float32)
        up_part = jnp.dot(rows_ref[...], up_ref[:, cols], preferred_element_type=jnp.float32)
        hidden_ref[:, cols] = (gate_part / (1.0 + jnp.exp(-gate_part)) * up_part).astype(jnp.bfloat16)
    half = first // 2

    for start in range(0, width, 1024):
        cols = slice(start, start + 1024)
        out = jnp.dot(hidden_ref[...], down_ref[:, cols], preferred_element_type=jnp.float32) * weight
        own_ref[:, cols] = out[:half].astype(jnp.bfloat16)
        at = half
        for other_ref in other_refs:
            other_ref[:, cols] = out[at : at + other_ref.shape[0]].astype(jnp.bfloat16)
            at += other_ref.shape[0]


def expert_rows(blocks, mine, w_gate, w_up, w_down, cuts):
    rows = sum(block.shape[0] for block in blocks)
    width, units = w_down.shape[1], w_gate.shape[1]
    return local(
        functools.partial(expert_body, len(blocks)),
        [(rows // 2, width), *((cut, width) for cut in cuts)],
        (mine, *blocks, w_gate, w_up, w_down),
        [pltpu.VMEM((rows, width), jnp.bfloat16), pltpu.VMEM((rows, units), jnp.bfloat16)],
        flops=6 * rows * width * units,
        bytes_accessed=2 * rows * width,
    )


def add_body(plan, count, rows, *refs):
    for out, blocks in zip(refs[count:], plan):
        for at, parts in enumerate(blocks):
            cut = [refs[ref][place * rows : (place + 1) * rows, :] for ref, place in parts]
            if len(cut) > 1:
                cut = [sum(part.astype(jnp.float32) for part in cut).astype(jnp.bfloat16)]
            out[at * rows : (at + 1) * rows, :] = cut[0]


def combine(wanted, pieces, rows, after=()):
    plan = [
        [
            [(ref, names.index(m)) for ref, (names, _) in enumerate(pieces) if m in names]
            for m in blocks
        ]
        for blocks in wanted
    ]
    arrays = [array for _, array in pieces]
    width = arrays[0].shape[1]
    outs = local(
        functools.partial(add_body, plan, len(arrays) + len(after), rows),
        [(len(blocks) * rows, width) for blocks in wanted],
        arrays,
        limit=4,
        after=after,
    )
    return list(zip(wanted, outs))


def spread(hidden_in, routes, scores, w_gate, w_up, w_down):
    rows = hidden_in.shape[0]
    experts = lax.axis_size("dev")
    devices = experts * lax.axis_size("sec")
    lanes = jnp.arange(128)
    mine = (lanes % experts == lax.axis_index("dev")) & (lanes < TERMS * experts)
    mine = mine.astype(jnp.float32)[None, :]

    def send(link, piece):
        names, array = piece
        return tuple(m ^ link for m in names), swap(array, link, devices)

    def shares(pieces, *cuts):
        names = sum((tuple(names) for names, _ in pieces), ())
        here = [array for _, array in pieces]
        there = [swap(array, CORE, devices) for array in here]
        cuts = cuts or (len(names),)
        own, *others = expert_rows(here + there, mine, *weights, [cut * rows for cut in cuts])
        starts = [sum(cuts[:at]) for at in range(len(cuts))]
        parts = [tuple(m ^ CORE for m in names[at : at + cut]) for at, cut in zip(starts, cuts)]
        return [(names, own), *zip(parts, others)]

    def tie(*pieces):
        arrays = lax.optimization_barrier(tuple(array for _, array in pieces))
        return [(names, array) for (names, _), array in zip(pieces, arrays)]

    def sums(pieces, *beside):
        own, other, *beside = tie(*shares(pieces), *beside)
        return [own, send(CORE, other)], *beside

    start = [0], prepare(hidden_in, routes, scores, experts, mine)
    zb, x, y, xy, za = [send(link, start) for link in (ZB, X, Y, X | Y, ZA)]
    weights, token = fetch((w_gate[0], w_up[0], w_down[0]), start[1])
    near, zs, ps = combine(
        [[0, ZA, X, Y, ZB, X | Y], [ZA, ZB], [X | Y, ZB]], [start, za, x, y, zb, xy], rows, [token]
    )

    near, xs, ys, pz, xyb = sums(
        [near], send(X, zs), send(Y, zs), send(ZA, ps), send(X | Y, zb)
    )
    side, rest, zab = combine(
        [[X | ZA, X | ZB, Y | ZA, Y | ZB, X | Y | ZA], [ZA | ZB, X | Y | ZB], [ZA | ZB]],
        [xs, ys, pz, xyb],
        rows,
    )
    side, *got = sums([side], send(X, zab), send(Y, zab), send(ZA, xyb))
    (far,) = combine([[X | ZA | ZB, Y | ZA | ZB, X | Y | ZA | ZB]], got, rows)
    x, y, xya = combine([[X | ZA, X | ZB], [Y | ZA, Y | ZB], [X | Y | ZA]], side, rows)
    own, *others = shares([far, rest], 1, 2, 2)
    own, x, y, xya = tie(own, send(X, x), send(Y, y), send(ZA, xya))
    far = [own, *(send(CORE, other) for other in others)]
    (x,) = combine([[ZA, ZB]], [x, y], rows)

    xyab, xa, ya = combine(
        [[X | Y | ZA | ZB], [X | ZA | ZB], [Y | ZA | ZB]], far, rows, [x[1]]
    )
    xyab, xa, ya = send(ZA, xyab), send(X, xa), send(Y, ya)
    (xyb,) = combine([[X | Y | ZB]], [*far, xyab], rows)
    xyb = send(X | Y, xyb)
    (zab,) = combine([[ZA | ZB]], [*far, xa, ya], rows)
    got = x, xya, xyb, send(ZA, zab)
    ends = combine([[ZB]], [*near, *got], rows)
    ends += combine([[X], [Y], [ZA], [X | Y]], [*near, *got], rows)
    ends = [send(piece[0][0], piece) for piece in ends]
    return combine([[0]], [*ends, *near], rows)[0][1]


def dispatch(hidden_in, routes, scores, w_gate, w_up, w_down):
    rows_dev, model_width = hidden_in.shape
    top_k = routes.shape[1]
    experts = lax.axis_size("dev")
    slots_dev = 2 * rows_dev * top_k // experts
    slot_rows = experts * slots_dev
    normed = normalise(hidden_in)
    shares = scores / jnp.sum(scores, -1, keepdims=True)
    chosen = routes.reshape(-1)
    onehot = (chosen[:, None] == jnp.arange(experts, dtype=jnp.int32)[None, :]).astype(jnp.int32)
    before = jnp.cumsum(onehot, 0) - onehot
    position = jnp.sum(before * onehot, 1)
    target = (chosen * slots_dev + position).reshape(rows_dev, top_k)
    places = jnp.arange(slot_rows, dtype=jnp.int32)
    picker = jnp.any(target[None, :, :] == places[:, None, None], -1).astype(jnp.bfloat16)
    outgoing = jnp.dot(picker, normed, preferred_element_type=jnp.float32).astype(jnp.bfloat16)
    outgoing = outgoing.reshape(experts, slots_dev, model_width)
    arrived = lax.all_to_all(outgoing, "dev", split_axis=0, concat_axis=0, tiled=True).reshape(
        slot_rows, model_width
    )
    paired = lax.all_gather(arrived, "sec", axis=0, tiled=True)
    result = lax.psum_scatter(
        expert(paired, w_gate[0], w_up[0], w_down[0]).astype(jnp.bfloat16),
        "sec",
        scatter_dimension=0,
        tiled=True,
    )
    expert_out = result.reshape(experts, slots_dev, model_width)
    returned = lax.all_to_all(expert_out, "dev", split_axis=0, concat_axis=0, tiled=True).reshape(
        slot_rows, model_width
    )
    picked = jnp.take(returned, target.reshape(-1), axis=0).reshape(rows_dev, top_k, model_width)
    combined = jnp.einsum("rk,rkd->rd", shares, picked.astype(jnp.float32))
    return combined.astype(jnp.bfloat16)


def on_device(hidden_in, routes, scores, *weights):
    experts, halves = lax.axis_size("dev"), lax.axis_size("sec")
    roomy = 2 * routes.shape[1] >= experts
    plan = spread if roomy and (halves, experts) == (2, 16) else dispatch
    return plan(hidden_in, routes, scores, *weights)


def solution(mesh):
    placed = (
        P(("sec", "dev"), None),
        P(("sec", "dev"), None),
        P(("sec", "dev"), None),
        P("dev", None, "sec"),
        P("dev", None, "sec"),
        P("dev", "sec", None),
    )
    return jax.shard_map(
        on_device, mesh=mesh, in_specs=placed, out_specs=P(("sec", "dev"), None), check_vma=False
    )
```
